512 devices in a mesh: cable: 32 (over y, x), pair: 16 (over z, core).
Axes of the slice: x: 4, y: 8, z: 8, core: 2. Of those that a mesh axis runs over, the one named last changes fastest.
Arguments:
- raw_strain: bfloat16 [4096, 2048], P('cable', 'pair'), may hold values from -40 to 40
- smooth_taps: float32 [101], replicated, may hold values from 0.02 to 1
- partner_block: int32 [32, 16], P('cable'), may hold values from 0 to 31, as said below
- chan_offset: int32 [32, 16], P('cable'), may hold values from 0 to 127
- pair_count: int32 [32], P('cable'), may hold values from 1 to 16
Outputs:
- correlations: float32 [32, 16, 401, 128], P('cable', 'pair')
The draws below stay inside these ranges and needn't reach their ends.
Inputs may be any that keep to these rules, and one draw needn't show every extreme that they name: `partner_block`: each entry lies within 2 of its row's block index.
All inputs are finite; a program needn't handle non-finite values.
Results may differ from the reference program's by a relative error of at most 0.014.
Values may be sent and summed in bfloat16 or wider, within the bound.
No kernel may reach another device: no remote copies, remote signals or barrier semaphores. Data moves between devices by JAX's collectives and lax.ppermute only.
A program may use at most 64 MiB of HBM per device.

```python
import math
import jax
import jax.numpy as jnp
from jax import lax

BLK = 128
HW = 50
LAG = 200
REACH = 2
NT = 2048
NBLK = 32
NCH = 4096
PMAX = 16


def draw_raw_strain(key, part):
    key = jax.random.fold_in(key, 11)
    first_key, second_key, third_key = jax.random.split(key, 3)
    noise = jnp.clip(jax.random.normal(first_key, (NCH, NT), jnp.float32), -4.0, 4.0)
    lowest, highest = (0.25, 4.0)
    channel_scale = jnp.exp(jax.random.uniform(second_key, (NCH, 1), jnp.float32, math.log(0.5), math.log(2.0)))
    segment_scale = jnp.exp(jax.random.uniform(third_key, (NCH, NT // 16), jnp.float32, math.log(lowest), math.log(highest)))
    segment_scale = jnp.repeat(segment_scale, 16, axis=1)
    return (noise * channel_scale * segment_scale).astype(jnp.bfloat16)


def draw_partner_block(key, part):
    key = jax.random.fold_in(key, 23)
    offsets = jax.random.randint(key, (NBLK, PMAX), -REACH, REACH + 1, dtype=jnp.int32)
    block_rows = jnp.arange(NBLK, dtype=jnp.int32)[:, None]
    return jnp.clip(block_rows + offsets, 0, NBLK - 1).astype(jnp.int32)


def draw_pair_count(key, part):
    key = jax.random.fold_in(key, 37)
    first_key, second_key = jax.random.split(key)
    counts = jax.random.randint(first_key, (NBLK,), 1, PMAX + 1, dtype=jnp.int32)
    chosen = jax.random.randint(second_key, (), 0, NBLK, dtype=jnp.int32)
    return jnp.where(jnp.arange(NBLK, dtype=jnp.int32) == chosen, PMAX, counts).astype(jnp.int32)


def set_ends(drawn, key, smallest, top_value):
    longest = drawn.shape.index(max(drawn.shape))
    spots = []
    for shift in (0, 1):
        where = [jax.random.randint(jax.random.fold_in(key, axis), (), 0, length) for axis, length in enumerate(drawn.shape)]
        where[longest] = (where[longest] + shift) % drawn.shape[longest]
        spots.append(tuple(where))
    return drawn.at[spots[0]].set(smallest).at[spots[1]].set(top_value)


def setup_inputs(seed: int = 0) -> dict:
    key_of = jax.random.split(jax.random.key(seed), 6)
    raw_strain = draw_raw_strain(jax.random.fold_in(key_of[5], 71), 0)
    smooth_taps = jnp.clip(jnp.exp(jax.random.uniform(key_of[1], (2 * HW + 1,), jnp.float32, math.log(0.02), math.log(1.0))), 0.02, 1.0)
    partner_block = draw_partner_block(jax.random.fold_in(key_of[5], 71), 0)
    chan_offset = set_ends(jax.random.randint(key_of[3], (NBLK, PMAX), 0, BLK), jax.random.fold_in(key_of[3], 1), 0, BLK - 1).astype(jnp.int32)
    pair_count = draw_pair_count(jax.random.fold_in(key_of[5], 71), 0)
    return {"raw_strain": raw_strain, "smooth_taps": smooth_taps, "partner_block": partner_block, "chan_offset": chan_offset, "pair_count": pair_count}


EPSILON = 1e-05

def reference(raw_strain, smooth_taps, partner_block, chan_offset, pair_count):
    values = raw_strain.astype(jnp.float32)
    padded = jnp.pad(jnp.abs(values), ((0, 0), (HW, HW)))
    smoothed = lax.conv_general_dilated(padded[:, None, :], smooth_taps[None, None, :], (1,), 'VALID', precision=lax.Precision.HIGHEST)[:, 0, :]
    envelope = smoothed / jnp.sum(smooth_taps)
    unit_series = (values / (envelope + EPSILON)).astype(jnp.bfloat16)
    extended = jnp.concatenate([unit_series.astype(jnp.float32), jnp.zeros((BLK, NT), jnp.float32)], 0)
    fft_length = ((NT + LAG) // 128 + 1) * 128
    spectra = jnp.fft.rfft(extended, n=fft_length, axis=1)
    lag_index = (jnp.arange(2 * LAG + 1, dtype=jnp.int32) - LAG) % fft_length
    channel_steps = jnp.arange(BLK, dtype=jnp.int32)

    def one_block(block_id):
        own_spectrum = lax.dynamic_slice_in_dim(spectra, block_id * BLK, BLK, 0)
        row_index = partner_block[block_id][:, None] * BLK + chan_offset[block_id][:, None] + channel_steps[None, :]
        partner_spectra = spectra[row_index]
        full_series = jnp.fft.irfft(jnp.conj(own_spectrum)[None] * partner_spectra, n=fft_length, axis=2)
        picked_lags = jnp.take(full_series, lag_index, axis=2)
        live_slots = (jnp.arange(PMAX, dtype=jnp.int32) < pair_count[block_id]).astype(jnp.float32)
        return jnp.transpose(picked_lags, (0, 2, 1)) * (live_slots[:, None, None] / math.sqrt(NT))
    return lax.map(one_block, jnp.arange(NBLK, dtype=jnp.int32))
```

```python
import math

import jax
import jax.numpy as jnp
import ml_dtypes
import numpy as np
from jax import lax
from jax.experimental import pallas as pl
from jax.experimental.pallas import tpu as pltpu
from jax.sharding import PartitionSpec as P

LAG = 200
REACH = 2
EPSILON = 1e-05
FREQ = 128
LAG_PAD = 512


def transform_tables(samples):
    length = -(-(samples + LAG) // (2 * FREQ)) * 2 * FREQ
    steps = length // 2 // FREQ
    theta = 2 * np.pi * (np.arange(length // 2) + 0.5) / length
    angle = np.outer(np.arange(samples), theta)
    cosine = np.cos(angle).reshape(samples, steps, FREQ)
    sine = np.sin(angle).reshape(samples, steps, FREQ)
    forward = np.concatenate([cosine, sine], 2).transpose(1, 0, 2)
    angle = np.outer(theta, np.arange(LAG_PAD) - LAG)
    weight = 2.0 / length / math.sqrt(samples)
    cosine = (np.cos(angle) * weight).reshape(steps, FREQ, LAG_PAD)
    sine = (np.sin(angle) * weight).reshape(steps, FREQ, LAG_PAD)
    backward = np.concatenate([cosine, sine], 1)
    return forward.astype(ml_dtypes.bfloat16), backward.astype(ml_dtypes.bfloat16)


def correlate_kernel(raw_ref, taps_ref, live_ref, forward_ref, backward_ref, out_ref, unit_ref):
    pieces, rows, width = raw_ref.shape
    half = rows // 2
    span = taps_ref.shape[1]
    taps = taps_ref[...].astype(jnp.bfloat16).astype(jnp.float32)
    total = jnp.sum(taps)
    band = pltpu.roll(
        jnp.broadcast_to(taps, (2 * width, span)), 0, 1, stride=1, stride_axis=0
    ).astype(jnp.bfloat16)
    outside = jnp.zeros((rows, width), jnp.bfloat16)
    for first in range(0, pieces, 2):
        parts = [
            raw_ref[p] if 0 <= p < pieces else outside for p in range(first - 1, first + 3)
        ]
        smoothed = lax.dot_general(
            jnp.abs(jnp.concatenate(parts, 1)),
            band,
            (((1,), (1,)), ((), ())),
            preferred_element_type=jnp.float32,
        )
        values = jnp.concatenate(parts[1:3], 1).astype(jnp.float32)
        unit_ref[:, first * width : (first + 2) * width] = (
            values / (smoothed / total + EPSILON)
        ).astype(jnp.bfloat16)
    result = jnp.zeros((half, LAG_PAD), jnp.float32)
    for step in range(forward_ref.shape[0]):
        spectra = jnp.dot(unit_ref[...], forward_ref[step], preferred_element_type=jnp.float32)
        own_cos, own_sin = spectra[:half, :FREQ], spectra[:half, FREQ:]
        far_cos, far_sin = spectra[half:, :FREQ], spectra[half:, FREQ:]
        product = jnp.concatenate(
            [own_cos * far_cos + own_sin * far_sin, own_cos * far_sin - own_sin * far_cos], 1
        ).astype(jnp.bfloat16)
        result = result + jnp.dot(
            product, backward_ref[step], preferred_element_type=jnp.float32
        )
    out_ref[...] = (result * live_ref[0]).T[: out_ref.shape[0]]


def correlate(raw, smooth_taps, live):
    pieces, rows, width = raw.shape
    forward, backward = transform_tables(pieces * width)
    lead = width - (smooth_taps.shape[0] - 1) // 2
    taps = jnp.pad(smooth_taps, (lead, 4 * width - lead - smooth_taps.shape[0]))[None]
    whole = pl.BlockSpec(memory_space=pltpu.VMEM)
    return pl.pallas_call(
        correlate_kernel,
        out_shape=jax.ShapeDtypeStruct((2 * LAG + 1, rows // 2), jnp.float32),
        in_specs=[whole, whole, pl.BlockSpec(memory_space=pltpu.SMEM), whole, whole],
        out_specs=whole,
        scratch_shapes=[pltpu.VMEM((rows, pieces * width), jnp.bfloat16)],
        compiler_params=pltpu.CompilerParams(vmem_limit_bytes=40 << 20),
    )(raw, taps, live, jnp.asarray(forward), jnp.asarray(backward))


def from_behind(value, axis, steps):
    count = lax.axis_size(axis)
    first, last = (max(0, -steps), min(count, count - steps))
    return lax.ppermute(value, axis, [(source, source + steps) for source in range(first, last)])


def per_device(raw_strain, smooth_taps, partner_block, chan_offset, pair_count):
    block_rows = raw_strain.shape[0]
    cable_place = lax.axis_index("cable")
    pair_place = lax.axis_index("pair")
    lower = [from_behind(raw_strain, "cable", d) for d in range(REACH, 0, -1)]
    upper = [from_behind(raw_strain, "cable", -d) for d in range(1, REACH + 2)]
    window = jnp.concatenate(lower + [raw_strain] + upper, 0)
    starts = (partner_block[0] - cable_place + REACH) * block_rows + chan_offset[0]
    picked = [
        jnp.concatenate(
            [raw_strain, lax.dynamic_slice_in_dim(window, starts[s], block_rows, 0)], 0
        )
        for s in range(starts.shape[0])
    ]
    records = lax.all_to_all(jnp.stack(picked, 0), "pair", 0, 0)
    live = (pair_place < pair_count[0]).astype(jnp.float32)
    return correlate(records, smooth_taps, live[None])[None, None]


def solution(mesh):
    in_specs = (P("cable", "pair"), P(), P("cable", None), P("cable", None), P("cable"))
    out_specs = P("cable", "pair", None, None)
    return jax.shard_map(
        per_device, mesh=mesh, in_specs=in_specs, out_specs=out_specs, check_vma=False
    )
```

```python
import math

import jax
import jax.numpy as jnp
import ml_dtypes
import numpy as np
from jax import lax
from jax.experimental import pallas as pl
from jax.experimental.pallas import tpu as pltpu
from jax.sharding import PartitionSpec as P

LAG = 200
REACH = 2
EPSILON = 1e-05
WIDE = 256
LAG_PAD = 512


def transform_tables(samples):
    length = -(-(samples + LAG) // WIDE) * WIDE
    theta = 2 * np.pi * (np.arange(length // 2) + 0.5) / length
    forward = np.outer(np.arange(samples // 2) + 0.5, theta)
    backward = np.outer(theta, np.arange(LAG_PAD) - LAG)
    weight = 2.0 / length / math.sqrt(samples)
    tables = (
        np.cos(forward),
        np.sin(forward),
        np.cos(backward) * weight,
        np.sin(backward) * weight,
    )
    return [jnp.asarray(table.astype(ml_dtypes.bfloat16)) for table in tables]


def correlate_kernel(
    raw_ref,
    taps_hbm,
    cos_hbm,
    sin_hbm,
    back_cos_hbm,
    back_sin_hbm,
    out_hbm,
    taps_ref,
    cos_ref,
    sin_ref,
    back_cos_ref,
    back_sin_ref,
    row_ref,
    unit_ref,
    even_ref,
    odd_ref,
    real_ref,
    imag_ref,
    out_ref,
    copied,
):
    pieces, rows, width = raw_ref.shape
    half = rows // 2
    frequencies = cos_ref.shape[1]
    starts = range(0, frequencies, WIDE)
    taps_copy = pltpu.make_async_copy(taps_hbm, taps_ref, copied.at[0])
    taps_copy.start()
    copies = []
    for start in starts:
        part = pl.ds(start, min(WIDE, frequencies - start))
        for source, target in ((cos_hbm, cos_ref), (sin_hbm, sin_ref)):
            copies.append(
                pltpu.make_async_copy(
                    source.at[:, part], target.at[:, part], copied.at[1 + len(copies)]
                )
            )
    for source, target in ((back_cos_hbm, back_cos_ref), (back_sin_hbm, back_sin_ref)):
        copies.append(pltpu.make_async_copy(source, target, copied.at[1 + len(copies)]))
    for copy in copies:
        copy.start()

    row_ref[...] = jnp.zeros_like(row_ref)
    lead = width - (taps_ref.shape[1] - 1) // 2
    taps_copy.wait()
    row_ref[:, lead : lead + taps_ref.shape[1]] = taps_ref[...]
    taps = row_ref[...].astype(jnp.bfloat16).astype(jnp.float32)
    scale = 1.0 / jnp.sum(taps)
    band = pltpu.roll(
        jnp.broadcast_to(taps, (WIDE, row_ref.shape[1])), 0, 1, stride=1, stride_axis=0
    ).astype(jnp.bfloat16)
    outside = jnp.zeros((rows, width), jnp.bfloat16)
    for first in range(0, pieces, 2):
        parts = [
            raw_ref[p] if 0 <= p < pieces else outside for p in range(first - 1, first + 3)
        ]
        smoothed = lax.dot_general(
            jnp.abs(jnp.concatenate(parts, 1)),
            band,
            (((1,), (1,)), ((), ())),
            preferred_element_type=jnp.float32,
        )
        values = jnp.concatenate(parts[1:3], 1).astype(jnp.float32)
        unit_ref[:, first * width : first * width + WIDE] = (
            values / (smoothed * scale + EPSILON)
        ).astype(jnp.bfloat16)

    mirror = (
        lax.broadcasted_iota(jnp.int32, (WIDE, WIDE), 0)
        + lax.broadcasted_iota(jnp.int32, (WIDE, WIDE), 1)
        == WIDE - 1
    ).astype(jnp.bfloat16)
    middle = even_ref.shape[1]
    for start in range(0, middle, WIDE):
        mirrored = jnp.dot(
            unit_ref[:, middle - start - WIDE : middle - start],
            mirror,
            preferred_element_type=jnp.float32,
        )
        later = unit_ref[:, middle + start : middle + start + WIDE].astype(jnp.float32)
        even_ref[:, start : start + WIDE] = (later + mirrored).astype(jnp.bfloat16)
        odd_ref[:, start : start + WIDE] = (later - mirrored).astype(jnp.bfloat16)

    for step, start in enumerate(starts):
        stop = min(start + WIDE, frequencies)
        copies[2 * step].wait()
        copies[2 * step + 1].wait()
        cosine = jnp.dot(
            even_ref[...], cos_ref[:, start:stop], preferred_element_type=jnp.float32
        )
        sine = jnp.dot(odd_ref[...], sin_ref[:, start:stop], preferred_element_type=jnp.float32)
        own_cos, far_cos = cosine[:half], cosine[half:]
        own_sin, far_sin = sine[:half], sine[half:]
        real_ref[:, start:stop] = (own_cos * far_cos + own_sin * far_sin).astype(jnp.bfloat16)
        imag_ref[:, start:stop] = (own_cos * far_sin - own_sin * far_cos).astype(jnp.bfloat16)
    copies[-2].wait()
    copies[-1].wait()
    result = jnp.dot(
        real_ref[...], back_cos_ref[...], preferred_element_type=jnp.float32
    ) + jnp.dot(imag_ref[...], back_sin_ref[...], preferred_element_type=jnp.float32)
    out_ref[...] = result.T[: out_ref.shape[0]]
    written = pltpu.make_async_copy(out_ref, out_hbm.at[:, 0], copied.at[0])
    written.start()
    written.wait()


def correlate(raw, smooth_taps):
    pieces, rows, width = raw.shape
    samples = pieces * width
    tables = transform_tables(samples)
    vmem = pl.BlockSpec(memory_space=pltpu.VMEM)
    hbm = pl.BlockSpec(memory_space=pltpu.HBM)
    frequencies = tables[0].shape[1]
    copies = 2 * -(-frequencies // WIDE) + 2
    return pl.pallas_call(
        correlate_kernel,
        out_shape=jax.ShapeDtypeStruct((2 * LAG + 1, 1, rows // 2), jnp.float32),
        in_specs=[vmem] + [hbm] * 5,
        out_specs=hbm,
        scratch_shapes=[pltpu.VMEM((1, smooth_taps.shape[0]), jnp.float32)]
        + [pltpu.VMEM(table.shape, jnp.bfloat16) for table in tables]
        + [
            pltpu.VMEM((1, 2 * WIDE), jnp.float32),
            pltpu.VMEM((rows, samples), jnp.bfloat16),
            pltpu.VMEM((rows, samples // 2), jnp.bfloat16),
            pltpu.VMEM((rows, samples // 2), jnp.bfloat16),
            pltpu.VMEM((rows // 2, frequencies), jnp.bfloat16),
            pltpu.VMEM((rows // 2, frequencies), jnp.bfloat16),
            pltpu.VMEM((2 * LAG + 1, rows // 2), jnp.float32),
            pltpu.SemaphoreType.DMA((1 + copies,)),
        ],
        compiler_params=pltpu.CompilerParams(vmem_limit_bytes=56 << 20),
    )(raw, smooth_taps[None], *tables)


def pick_kernel(start_ref, window_ref, out_ref, wide_ref):
    slots, rows = out_ref.shape[0], out_ref.shape[1] // 2
    window_rows = window_ref.shape[0]
    wide_ref[:window_rows] = window_ref[...].astype(jnp.float32)
    wide_ref[window_rows:] = jnp.zeros_like(wide_ref[window_rows:])
    own = window_ref[REACH * rows : (REACH + 1) * rows]
    for slot in range(slots):
        out_ref[slot, :rows] = own
        out_ref[slot, rows:] = wide_ref[pl.ds(start_ref[slot], rows)].astype(jnp.bfloat16)


def pick(starts, window, rows):
    window_rows, width = window.shape
    vmem = pl.BlockSpec(memory_space=pltpu.VMEM)
    smem = pl.BlockSpec(memory_space=pltpu.SMEM)
    return pl.pallas_call(
        pick_kernel,
        out_shape=jax.ShapeDtypeStruct((starts.shape[0], 2 * rows, width), jnp.bfloat16),
        in_specs=[smem, vmem],
        out_specs=vmem,
        scratch_shapes=[pltpu.VMEM((window_rows + rows, width), jnp.float32)],
        compiler_params=pltpu.CompilerParams(vmem_limit_bytes=8 << 20),
    )(starts, window)


def from_behind(value, axis, steps):
    count = lax.axis_size(axis)
    first, last = (max(0, -steps), min(count, count - steps))
    return lax.ppermute(value, axis, [(source, source + steps) for source in range(first, last)])


def per_device(raw_strain, smooth_taps, partner_block, chan_offset, pair_count):
    rows = raw_strain.shape[0]
    first_block = lax.axis_index("cable") - REACH
    lower = [from_behind(raw_strain, "cable", d) for d in range(REACH, 0, -1)]
    upper = [from_behind(raw_strain, "cable", -d) for d in range(1, REACH + 2)]
    window = jnp.concatenate(lower + [raw_strain] + upper, 0)
    starts = (partner_block[0] - first_block) * rows + chan_offset[0]
    live = jnp.arange(starts.shape[0], dtype=jnp.int32) < pair_count
    starts = jnp.where(live, starts, window.shape[0])
    window, starts = lax.optimization_barrier((window, starts))
    records = lax.all_to_all(pick(starts, window, rows), "pair", 0, 0)
    return correlate(records, smooth_taps).reshape(1, 1, 2 * LAG + 1, rows)


def solution(mesh):
    in_specs = (P("cable", "pair"), P(), P("cable", None), P("cable", None), P("cable"))
    out_specs = P("cable", "pair", None, None)
    return jax.shard_map(
        per_device, mesh=mesh, in_specs=in_specs, out_specs=out_specs, check_vma=False
    )
```

```python
import math

import jax
import jax.numpy as jnp
import ml_dtypes
import numpy as np
from jax import lax
from jax.experimental import pallas as pl
from jax.experimental.pallas import tpu as pltpu
from jax.sharding import PartitionSpec as P

LAG = 200
REACH = 2
EPSILON = 1e-05
WIDE = 256
LAG_PAD = 512
LANES = 128
F32 = jnp.float32
BF16 = jnp.bfloat16


def transform_tables(samples):
    length = -(-(samples + LAG) // WIDE) * WIDE
    theta = 2 * np.pi * (np.arange(length // 2) + 0.5) / length
    forward = np.outer(np.arange(samples // 2) + 0.5, theta)
    backward = np.outer(theta, np.arange(LAG_PAD) - LAG)
    weight = 2.0 / length / math.sqrt(samples)
    tables = (
        np.cos(forward),
        np.sin(forward),
        np.cos(backward) * weight,
        np.sin(backward) * weight,
    )
    return [jnp.asarray(table.astype(ml_dtypes.bfloat16)) for table in tables]


def smoothing_band(taps_ref, row_ref, width):
    row_ref[...] = jnp.zeros_like(row_ref)
    lead = width - (taps_ref.shape[1] - 1) // 2
    row_ref[:, lead : lead + taps_ref.shape[1]] = taps_ref[...]
    taps = row_ref[...].astype(BF16).astype(F32)
    band = pltpu.roll(
        jnp.broadcast_to(taps, (WIDE, row_ref.shape[1])), 0, 1, stride=1, stride_axis=0
    ).astype(BF16)
    return band, 1.0 / jnp.sum(taps)


def normalize(piece, pieces, rows, band, scale, unit_ref):
    width = unit_ref.shape[1] // pieces
    outside = jnp.zeros((rows, width), F32)
    for first in range(0, pieces, 2):
        parts = [piece(p) if 0 <= p < pieces else outside for p in range(first - 1, first + 3)]
        smoothed = lax.dot_general(
            jnp.abs(jnp.concatenate(parts, 1)).astype(BF16),
            band,
            (((1,), (1,)), ((), ())),
            preferred_element_type=F32,
        )
        values = jnp.concatenate(parts[1:3], 1)
        unit_ref[:, first * width : first * width + WIDE] = (
            values / (smoothed * scale + EPSILON)
        ).astype(BF16)


def fold(unit_ref, even_ref, odd_ref):
    mirror = (
        lax.broadcasted_iota(jnp.int32, (WIDE, WIDE), 0)
        + lax.broadcasted_iota(jnp.int32, (WIDE, WIDE), 1)
        == WIDE - 1
    ).astype(BF16)
    middle = even_ref.shape[1]
    for start in range(0, middle, WIDE):
        mirrored = jnp.dot(
            unit_ref[:, middle - start - WIDE : middle - start],
            mirror,
            preferred_element_type=F32,
        )
        later = unit_ref[:, middle + start : middle + start + WIDE].astype(F32)
        even_ref[:, start : start + WIDE] = (later + mirrored).astype(BF16)
        odd_ref[:, start : start + WIDE] = (later - mirrored).astype(BF16)


def own_kernel(
    raw_ref,
    taps_ref,
    cos_hbm,
    sin_hbm,
    own_cos_ref,
    own_sin_ref,
    cos_ref,
    sin_ref,
    band_ref,
    scale_ref,
    row_ref,
    unit_ref,
    even_ref,
    odd_ref,
    copied,
):
    pieces, rows, width = raw_ref.shape
    copies = [
        pltpu.make_async_copy(source, target, copied.at[place])
        for place, (source, target) in enumerate(((cos_hbm, cos_ref), (sin_hbm, sin_ref)))
    ]
    for copy in copies:
        copy.start()
    band, scale = smoothing_band(taps_ref, row_ref, width)
    band_ref[...] = band
    scale_ref[...] = jnp.broadcast_to(scale, scale_ref.shape)
    normalize(lambda p: raw_ref[p].astype(F32), pieces, rows, band, scale, unit_ref)
    fold(unit_ref, even_ref, odd_ref)
    spare = own_cos_ref.shape[1] - rows
    frequencies = cos_ref.shape[1]
    copies[0].wait()
    copies[1].wait()
    for part_ref, table_ref, spectrum_ref in (
        (even_ref, cos_ref, own_cos_ref),
        (odd_ref, sin_ref, own_sin_ref),
    ):
        for start in range(0, frequencies, WIDE):
            stop = min(start + WIDE, frequencies)
            spectrum = jnp.dot(
                part_ref[...], table_ref[:, start:stop], preferred_element_type=F32
            )
            for lane in range(start, stop, LANES):
                tile = spectrum[:, lane - start : lane - start + LANES]
                spectrum_ref[lane // LANES, :rows] = tile
                spectrum_ref[lane // LANES, rows:] = tile[:spare]


def own_spectra(records, smooth_taps, tables, spare):
    pieces, rows, width = records.shape
    samples = pieces * width
    frequencies = tables[0].shape[1]
    vmem = pl.BlockSpec(memory_space=pltpu.VMEM)
    hbm = pl.BlockSpec(memory_space=pltpu.HBM)
    spectrum = jax.ShapeDtypeStruct((frequencies // LANES, rows + spare, LANES), F32)
    return pl.pallas_call(
        own_kernel,
        out_shape=[spectrum, spectrum]
        + [jax.ShapeDtypeStruct(table.shape, BF16) for table in tables]
        + [
            jax.ShapeDtypeStruct((WIDE, 2 * WIDE), BF16),
            jax.ShapeDtypeStruct((1, WIDE), F32),
        ],
        in_specs=[vmem, vmem] + [hbm] * 2,
        out_specs=[vmem] * 6,
        scratch_shapes=[
            pltpu.VMEM((1, 2 * WIDE), F32),
            pltpu.VMEM((rows, samples), BF16),
            pltpu.VMEM((rows, samples // 2), BF16),
            pltpu.VMEM((rows, samples // 2), BF16),
            pltpu.SemaphoreType.DMA((2,)),
        ],
        compiler_params=pltpu.CompilerParams(vmem_limit_bytes=47 << 20),
    )(records, smooth_taps[None], *tables)


def far_kernel(
    start_ref,
    own_cos_ref,
    own_sin_ref,
    cos_ref,
    sin_ref,
    band_ref,
    scale_ref,
    *refs,
):
    run_refs = refs[:3]
    (
        back_cos_hbm,
        back_sin_hbm,
        out_ref,
        unit_ref,
        even_ref,
        odd_ref,
        far_cos_ref,
        far_sin_ref,
        real_ref,
        imag_ref,
        back_cos_ref,
        back_sin_ref,
        copied,
    ) = refs[3:]
    copies = [
        pltpu.make_async_copy(back_cos_hbm, back_cos_ref, copied.at[0]),
        pltpu.make_async_copy(back_sin_hbm, back_sin_ref, copied.at[1]),
    ]
    for copy in copies:
        copy.start()
    _, pieces, share, _ = run_refs[0].shape
    block_rows = share * pieces
    blocks = [(ref, place) for ref in run_refs for place in range(ref.shape[0])]
    rows = len(blocks) * share
    frequencies = cos_ref.shape[1]
    inside = (lax.axis_size("cable") + REACH - lax.axis_index("cable")) * share
    within = lax.broadcasted_iota(jnp.int32, (rows, run_refs[0].shape[3]), 0) < inside
    normalize(
        lambda p: jnp.where(
            within,
            jnp.concatenate([ref[place, p].astype(F32) for ref, place in blocks], 0),
            0.0,
        ),
        pieces,
        rows,
        band_ref[...],
        scale_ref[...],
        unit_ref,
    )
    fold(unit_ref, even_ref, odd_ref)
    for start in range(0, frequencies, WIDE):
        stop = min(start + WIDE, frequencies)
        far_cos_ref[:, start:stop] = jnp.dot(
            even_ref[...], cos_ref[:, start:stop], preferred_element_type=F32
        )
        far_sin_ref[:, start:stop] = jnp.dot(
            odd_ref[...], sin_ref[:, start:stop], preferred_element_type=F32
        )

    slots = start_ref.shape[0]
    first = lax.axis_index("pair") * share
    place = first + lax.broadcasted_iota(jnp.int32, (share, frequencies), 0)
    pair = []
    for slot in range(slots):
        start = start_ref[slot]
        live = (start >= 0).astype(F32)
        start = jnp.maximum(start, 0)
        block = lax.div(start, block_rows)
        offset = lax.rem(start, block_rows)
        lower = pl.ds(pl.multiple_of(block * share, share), share)
        upper = pl.ds(pl.multiple_of(block * share + share, share), share)
        own = pl.ds(lax.rem(first - offset + block_rows, block_rows), share)
        before = place >= offset
        far_cos = jnp.where(before, far_cos_ref[lower], far_cos_ref[upper]) * live
        far_sin = jnp.where(before, far_sin_ref[lower], far_sin_ref[upper]) * live
        tiles = range(frequencies // LANES)
        own_cos = jnp.concatenate([own_cos_ref[tile, own] for tile in tiles], 1)
        own_sin = jnp.concatenate([own_sin_ref[tile, own] for tile in tiles], 1)
        pair.append(
            (own_cos * far_cos + own_sin * far_sin, own_cos * far_sin - own_sin * far_cos)
        )
        if len(pair) * share == 16:
            begin = (slot + 1) * share - 16
            real_ref[begin : begin + 16] = jnp.concatenate([p[0] for p in pair], 0).astype(BF16)
            imag_ref[begin : begin + 16] = jnp.concatenate([p[1] for p in pair], 0).astype(BF16)
            pair = []
    for copy in copies:
        copy.wait()
    result = jnp.dot(real_ref[...], back_cos_ref[...], preferred_element_type=F32) + jnp.dot(
        imag_ref[...], back_sin_ref[...], preferred_element_type=F32
    )
    for slot in range(slots):
        out_ref[slot] = jnp.concatenate(
            [
                result[slot * share : (slot + 1) * share, lane : lane + LANES]
                for lane in range(0, LAG_PAD, LANES)
            ],
            0,
        ).astype(BF16)


def far_products(starts, own, runs, tables):
    _, pieces, share, width = runs[0].shape
    slots = starts.shape[0]
    samples = pieces * width
    rows = sum(run.shape[0] for run in runs) * share
    frequencies = own[2].shape[1]
    vmem = pl.BlockSpec(memory_space=pltpu.VMEM)
    smem = pl.BlockSpec(memory_space=pltpu.SMEM)
    hbm = pl.BlockSpec(memory_space=pltpu.HBM)
    return pl.pallas_call(
        far_kernel,
        out_shape=jax.ShapeDtypeStruct((slots, share * LAG_PAD // LANES, LANES), BF16),
        in_specs=[smem] + [vmem] * (len(own) + len(runs)) + [hbm] * 2,
        out_specs=vmem,
        scratch_shapes=[
            pltpu.VMEM((rows, samples), BF16),
            pltpu.VMEM((rows, samples // 2), BF16),
            pltpu.VMEM((rows, samples // 2), BF16),
            pltpu.VMEM((rows, frequencies), F32),
            pltpu.VMEM((rows, frequencies), F32),
            pltpu.VMEM((slots * share, frequencies), BF16),
            pltpu.VMEM((slots * share, frequencies), BF16),
            pltpu.VMEM(tables[0].shape, BF16),
            pltpu.VMEM(tables[1].shape, BF16),
            pltpu.SemaphoreType.DMA((2,)),
        ],
        compiler_params=pltpu.CompilerParams(vmem_limit_bytes=44 << 20),
    )(starts, *own, *runs, *tables)


def place_kernel(start_ref, sent_ref, out_hbm, out_ref, copied):
    senders, rows, lanes = sent_ref.shape
    share = rows * lanes // LAG_PAD
    block_rows = senders * share
    offset = lax.rem(jnp.maximum(start_ref[lax.axis_index("pair")], 0), block_rows)
    turn = lax.rem(block_rows - offset, block_rows)
    total = out_ref.shape[0]
    for step in range(LAG_PAD // lanes):
        values = jnp.concatenate(
            [
                sent_ref[sender].astype(F32)[step * share : (step + 1) * share]
                for sender in range(senders)
            ],
            0,
        ).T
        stop = min(total, (step + 1) * lanes)
        out_ref[step * lanes : stop] = pltpu.roll(values, turn, 1)[: stop - step * lanes]
    written = pltpu.make_async_copy(out_ref, out_hbm.at[:, 0], copied.at[0])
    written.start()
    written.wait()


def place_lags(starts, sent, rows):
    vmem = pl.BlockSpec(memory_space=pltpu.VMEM)
    smem = pl.BlockSpec(memory_space=pltpu.SMEM)
    hbm = pl.BlockSpec(memory_space=pltpu.HBM)
    return pl.pallas_call(
        place_kernel,
        out_shape=jax.ShapeDtypeStruct((2 * LAG + 1, 1, rows), F32),
        in_specs=[smem, vmem],
        out_specs=hbm,
        scratch_shapes=[
            pltpu.VMEM((2 * LAG + 1, rows), F32),
            pltpu.SemaphoreType.DMA((1,)),
        ],
        compiler_params=pltpu.CompilerParams(vmem_limit_bytes=8 << 20),
    )(starts, sent)


def from_behind(value, axis, steps, also=()):
    count = lax.axis_size(axis)
    first, last = (max(0, -steps), min(count, count - steps))
    pairs = [(source, source + steps) for source in range(first, last)]
    return lax.ppermute(value, axis, pairs + list(also))


def per_device(raw_strain, smooth_taps, partner_block, chan_offset, pair_count):
    rows = raw_strain.shape[0]
    share = rows // lax.axis_size("pair")
    first_block = lax.axis_index("cable") - REACH
    starts = (partner_block[0] - first_block) * rows + chan_offset[0]
    live = jnp.arange(starts.shape[0], dtype=jnp.int32) < pair_count
    starts = jnp.where(live, starts, -1)
    records = lax.all_gather(raw_strain, "pair", axis=0)
    records, starts = lax.optimization_barrier((records, starts))
    mine = lax.dynamic_slice_in_dim(records, lax.axis_index("pair") * share, share, 1)
    last = lax.axis_size("cable") - 1
    middle = jnp.stack([mine, from_behind(mine, "cable", -1, [(0, last)])], 0)
    lower = from_behind(middle, "cable", REACH, [(last, 1)])
    upper = from_behind(middle, "cable", -REACH)
    tables = transform_tables(records.shape[0] * records.shape[2])
    own = own_spectra(records, smooth_taps, tables[:2], share)
    products = far_products(starts, own, [lower, middle, upper], tables[2:])
    sent = lax.all_to_all(products, "pair", 0, 0)
    return place_lags(starts, sent, rows).reshape(1, 1, 2 * LAG + 1, rows)


def solution(mesh):
    in_specs = (P("cable", "pair"), P(), P("cable", None), P("cable", None), P("cable"))
    out_specs = P("cable", "pair", None, None)
    return jax.shard_map(
        per_device, mesh=mesh, in_specs=in_specs, out_specs=out_specs, check_vma=False
    )
```

```python
import math

import jax
import jax.numpy as jnp
import ml_dtypes
import numpy as np
from jax import lax
from jax.experimental import pallas as pl
from jax.experimental.pallas import tpu as pltpu
from jax.sharding import PartitionSpec as P

LAG = 200
REACH = 2
EPSILON = 1e-05
WIDE = 256
LAG_PAD = 512
LANES = 128
TABLE_LIMIT = 47
OWN_LIMIT = 44
FAR_LIMIT = 44
F32 = jnp.float32
BF16 = jnp.bfloat16


def transform_tables(samples):
    length = -(-(samples + LAG) // WIDE) * WIDE
    theta = 2 * np.pi * (np.arange(length // 2) + 0.5) / length
    forward = np.outer(np.arange(samples // 2) + 0.5, theta)
    backward = np.outer(theta, np.arange(LAG_PAD) - LAG)
    weight = 2.0 / length / math.sqrt(samples)
    tables = (
        np.cos(forward),
        np.sin(forward),
        np.cos(backward) * weight,
        np.sin(backward) * weight,
    )
    return [jnp.asarray(table.astype(ml_dtypes.bfloat16)) for table in tables]


def smoothing_band(row):
    taps = row.astype(BF16).astype(F32)
    band = pltpu.roll(
        jnp.broadcast_to(taps, (WIDE, row.shape[1])), 0, 1, stride=1, stride_axis=0
    ).astype(BF16)
    return band, 1.0 / jnp.sum(taps)


def normalize(parts, band, scale):
    rows, width = parts[0].shape
    outside = jnp.zeros((rows, width), F32)
    padded = [outside] + parts + [outside]
    firsts = range(0, len(parts), 2)
    smoothed = lax.dot_general(
        jnp.concatenate(
            [jnp.abs(jnp.concatenate(padded[p : p + 4], 1)).astype(BF16) for p in firsts], 0
        ),
        band,
        (((1,), (1,)), ((), ())),
        preferred_element_type=F32,
    )
    values = jnp.concatenate([jnp.concatenate(parts[p : p + 2], 1) for p in firsts], 0)
    return (values / (smoothed * scale + EPSILON)).astype(BF16)


def fold(unit, rows):
    mirror = (
        lax.broadcasted_iota(jnp.int32, (WIDE, WIDE), 0)
        + lax.broadcasted_iota(jnp.int32, (WIDE, WIDE), 1)
        == WIDE - 1
    ).astype(BF16)
    half = unit.shape[0] // 2
    mirrored = jnp.dot(unit[:half], mirror, preferred_element_type=F32)
    later = unit[half:].astype(F32)
    even, odd = [], []
    for start in range(0, half, rows):
        ahead = later[start : start + rows]
        behind = mirrored[half - start - rows : half - start]
        even.append((ahead + behind).astype(BF16))
        odd.append((ahead - behind).astype(BF16))
    return jnp.concatenate(even, 1), jnp.concatenate(odd, 1)


def table_kernel(
    row_ref, cos_hbm, sin_hbm, cos_ref, sin_ref, band_ref, scale_ref, copied
):
    copies = [
        pltpu.make_async_copy(cos_hbm, cos_ref, copied.at[0]),
        pltpu.make_async_copy(sin_hbm, sin_ref, copied.at[1]),
    ]
    for copy in copies:
        copy.start()
    band, scale = smoothing_band(row_ref[...])
    band_ref[...] = band
    scale_ref[...] = jnp.broadcast_to(scale, scale_ref.shape)
    for copy in copies:
        copy.wait()


def forward_tables(taps_row, tables):
    vmem = pl.BlockSpec(memory_space=pltpu.VMEM)
    hbm = pl.BlockSpec(memory_space=pltpu.HBM)
    return pl.pallas_call(
        table_kernel,
        out_shape=[jax.ShapeDtypeStruct(table.shape, BF16) for table in tables]
        + [
            jax.ShapeDtypeStruct((WIDE, 2 * WIDE), BF16),
            jax.ShapeDtypeStruct((1, WIDE), F32),
        ],
        in_specs=[vmem, hbm, hbm],
        out_specs=[vmem] * 4,
        scratch_shapes=[pltpu.SemaphoreType.DMA((2,))],
        compiler_params=pltpu.CompilerParams(vmem_limit_bytes=TABLE_LIMIT << 20),
    )(taps_row, *tables)


def own_kernel(
    raw_ref, cos_ref, sin_ref, band_ref, scale_ref, own_cos_ref, own_sin_ref
):
    pieces, rows, _ = raw_ref.shape
    even, odd = fold(
        normalize(
            [raw_ref[p].astype(F32) for p in range(pieces)], band_ref[...], scale_ref[...]
        ),
        rows,
    )
    spare = own_cos_ref.shape[1] - rows
    frequencies = cos_ref.shape[1]
    for part, table_ref, spectrum_ref in (
        (even, cos_ref, own_cos_ref),
        (odd, sin_ref, own_sin_ref),
    ):
        for start in range(0, frequencies, WIDE):
            stop = min(start + WIDE, frequencies)
            spectrum = jnp.dot(part, table_ref[:, start:stop], preferred_element_type=F32)
            for lane in range(start, stop, LANES):
                tile = spectrum[:, lane - start : lane - start + LANES]
                spectrum_ref[lane // LANES, :rows] = tile
                spectrum_ref[lane // LANES, rows:] = tile[:spare]


def own_spectra(records, shared, spare):
    rows = records.shape[1]
    frequencies = shared[0].shape[1]
    vmem = pl.BlockSpec(memory_space=pltpu.VMEM)
    spectrum = jax.ShapeDtypeStruct((frequencies // LANES, rows + spare, LANES), F32)
    return pl.pallas_call(
        own_kernel,
        out_shape=[spectrum, spectrum],
        in_specs=[vmem] * (1 + len(shared)),
        out_specs=[vmem] * 2,
        compiler_params=pltpu.CompilerParams(vmem_limit_bytes=OWN_LIMIT << 20),
    )(records, *shared)


def far_kernel(
    start_any,
    own_cos_ref,
    own_sin_ref,
    cos_ref,
    sin_ref,
    band_ref,
    scale_ref,
    *refs,
):
    run_refs = refs[:3]
    (
        back_cos_hbm,
        back_sin_hbm,
        out_ref,
        far_cos_ref,
        far_sin_ref,
        real_ref,
        imag_ref,
        back_cos_ref,
        back_sin_ref,
        start_ref,
        copied,
    ) = refs[3:]
    start_copy = pltpu.make_async_copy(start_any, start_ref, copied.at[2])
    start_copy.start()
    copies = [
        pltpu.make_async_copy(back_cos_hbm, back_cos_ref, copied.at[0]),
        pltpu.make_async_copy(back_sin_hbm, back_sin_ref, copied.at[1]),
    ]
    for copy in copies:
        copy.start()
    _, pieces, share, _ = run_refs[0].shape
    block_rows = share * pieces
    blocks = [(ref, place) for ref in run_refs for place in range(ref.shape[0])]
    rows = len(blocks) * share
    frequencies = cos_ref.shape[1]
    inside = (lax.axis_size("cable") + REACH - lax.axis_index("cable")) * share
    within = lax.broadcasted_iota(jnp.int32, (rows, run_refs[0].shape[3]), 0) < inside
    parts = [
        jnp.where(
            within,
            jnp.concatenate([ref[place, p].astype(F32) for ref, place in blocks], 0),
            0.0,
        )
        for p in range(pieces)
    ]
    even, odd = fold(normalize(parts, band_ref[...], scale_ref[...]), rows)
    for start in range(0, frequencies, WIDE):
        stop = min(start + WIDE, frequencies)
        far_cos_ref[:, start:stop] = jnp.dot(
            even, cos_ref[:, start:stop], preferred_element_type=F32
        )
        far_sin_ref[:, start:stop] = jnp.dot(
            odd, sin_ref[:, start:stop], preferred_element_type=F32
        )

    slots = start_ref.shape[0]
    first = lax.axis_index("pair") * share
    place = first + lax.broadcasted_iota(jnp.int32, (share, frequencies), 0)
    pair = []
    start_copy.wait()
    for slot in range(slots):
        start = jnp.maximum(start_ref[slot], 0)
        block = lax.div(start, block_rows)
        offset = lax.rem(start, block_rows)
        lower = pl.ds(pl.multiple_of(block * share, share), share)
        upper = pl.ds(pl.multiple_of(block * share + share, share), share)
        own = pl.ds(lax.rem(first - offset + block_rows, block_rows), share)
        before = place >= offset
        far_cos = jnp.where(before, far_cos_ref[lower], far_cos_ref[upper])
        far_sin = jnp.where(before, far_sin_ref[lower], far_sin_ref[upper])
        tiles = range(frequencies // LANES)
        own_cos = jnp.concatenate([own_cos_ref[tile, own] for tile in tiles], 1)
        own_sin = jnp.concatenate([own_sin_ref[tile, own] for tile in tiles], 1)
        pair.append(
            (own_cos * far_cos + own_sin * far_sin, own_cos * far_sin - own_sin * far_cos)
        )
        if len(pair) * share == 16:
            begin = (slot + 1) * share - 16
            real_ref[begin : begin + 16] = jnp.concatenate([p[0] for p in pair], 0).astype(BF16)
            imag_ref[begin : begin + 16] = jnp.concatenate([p[1] for p in pair], 0).astype(BF16)
            pair = []
    for copy in copies:
        copy.wait()
    result = jnp.dot(real_ref[...], back_cos_ref[...], preferred_element_type=F32) + jnp.dot(
        imag_ref[...], back_sin_ref[...], preferred_element_type=F32
    )
    tile = (share * LAG_PAD // LANES, LANES)
    last_lane = (lax.broadcasted_iota(jnp.int32, tile, 0) >= tile[0] - share) & (
        lax.broadcasted_iota(jnp.int32, tile, 1) == LANES - 1
    )
    for slot in range(slots):
        lags = jnp.concatenate(
            [
                result[slot * share : (slot + 1) * share, lane : lane + LANES]
                for lane in range(0, LAG_PAD, LANES)
            ],
            0,
        )
        start = start_ref[slot]
        offset = lax.rem(jnp.maximum(start, 0), block_rows).astype(F32)
        lags = jnp.where(start >= 0, lags, 0.0)
        out_ref[slot] = jnp.where(last_lane, offset, lags).astype(BF16)


def far_products(starts, own, runs, tables):
    share = runs[0].shape[2]
    slots = starts.shape[0]
    rows = sum(run.shape[0] for run in runs) * share
    frequencies = own[2].shape[1]
    vmem = pl.BlockSpec(memory_space=pltpu.VMEM)
    hbm = pl.BlockSpec(memory_space=pltpu.HBM)
    anywhere = pl.BlockSpec(memory_space=pl.ANY)
    return pl.pallas_call(
        far_kernel,
        out_shape=jax.ShapeDtypeStruct((slots, share * LAG_PAD // LANES, LANES), BF16),
        in_specs=[anywhere] + [vmem] * (len(own) + len(runs)) + [hbm] * 2,
        out_specs=vmem,
        scratch_shapes=[
            pltpu.VMEM((rows, frequencies), F32),
            pltpu.VMEM((rows, frequencies), F32),
            pltpu.VMEM((slots * share, frequencies), BF16),
            pltpu.VMEM((slots * share, frequencies), BF16),
            pltpu.VMEM(tables[0].shape, BF16),
            pltpu.VMEM(tables[1].shape, BF16),
            pltpu.SMEM((slots,), jnp.int32),
            pltpu.SemaphoreType.DMA((3,)),
        ],
        compiler_params=pltpu.CompilerParams(vmem_limit_bytes=FAR_LIMIT << 20),
    )(starts, *own, *runs, *tables)


def place_kernel(sent_ref, out_hbm, out_ref, copied):
    senders, rows, lanes = sent_ref.shape
    tiles = LAG_PAD // lanes
    share = rows // tiles
    values = [sent_ref[sender].astype(F32) for sender in range(senders)]
    lags = [
        jnp.concatenate([value[step * share : (step + 1) * share] for value in values], 0)
        for step in range(tiles)
    ]
    block_rows = senders * share
    row = lax.broadcasted_iota(jnp.int32, (block_rows, block_rows), 0)
    channel = lax.broadcasted_iota(jnp.int32, (block_rows, block_rows), 1)
    offset = lags[-1][:, lanes - 1 :].astype(jnp.int32)
    ahead = row - offset - channel
    turn = ((ahead == 0) | (ahead == -block_rows)).astype(BF16)
    total = out_ref.shape[0]
    written = []
    for step in range(tiles):
        span = pl.ds(step * lanes, min(total, (step + 1) * lanes) - step * lanes)
        out_ref[span] = lax.dot_general(
            lags[step].astype(BF16),
            turn,
            (((0,), (0,)), ((), ())),
            preferred_element_type=F32,
        )[: span.size]
        written.append(
            pltpu.make_async_copy(out_ref.at[span], out_hbm.at[span, 0], copied.at[step])
        )
        written[-1].start()
    for copy in written:
        copy.wait()


def place_lags(sent, rows):
    vmem = pl.BlockSpec(memory_space=pltpu.VMEM)
    hbm = pl.BlockSpec(memory_space=pltpu.HBM)
    return pl.pallas_call(
        place_kernel,
        out_shape=jax.ShapeDtypeStruct((2 * LAG + 1, 1, rows), F32),
        in_specs=[vmem],
        out_specs=hbm,
        scratch_shapes=[
            pltpu.VMEM((2 * LAG + 1, rows), F32),
            pltpu.SemaphoreType.DMA((LAG_PAD // LANES,)),
        ],
        compiler_params=pltpu.CompilerParams(vmem_limit_bytes=8 << 20),
    )(sent)


def from_behind(value, axis, steps, also=()):
    count = lax.axis_size(axis)
    first, last = (max(0, -steps), min(count, count - steps))
    pairs = [(source, source + steps) for source in range(first, last)]
    return lax.ppermute(value, axis, pairs + list(also))


def per_device(raw_strain, smooth_taps, partner_block, chan_offset, pair_count):
    rows = raw_strain.shape[0]
    share = rows // lax.axis_size("pair")
    first_block = lax.axis_index("cable") - REACH
    records = lax.all_gather(raw_strain, "pair", axis=0)
    mine = lax.dynamic_slice_in_dim(records, lax.axis_index("pair") * share, share, 1)
    tables = transform_tables(records.shape[0] * records.shape[2])
    mine, smooth_taps, partner_block, chan_offset, pair_count = lax.optimization_barrier(
        (mine, smooth_taps, partner_block, chan_offset, pair_count)
    )
    last = lax.axis_size("cable") - 1
    middle = jnp.stack([mine, from_behind(mine, "cable", -1, [(0, last)])], 0)
    starts = (partner_block[0] - first_block) * rows + chan_offset[0]
    live = jnp.arange(starts.shape[0], dtype=jnp.int32) < pair_count
    starts = jnp.where(live, starts, -1)
    lead = records.shape[2] - (smooth_taps.shape[0] - 1) // 2
    taps_row = jnp.pad(smooth_taps, (lead, 2 * WIDE - lead - smooth_taps.shape[0]))[None]
    middle, starts, taps_row = lax.optimization_barrier((middle, starts, taps_row))
    shared = forward_tables(taps_row, tables[:2])
    lower = from_behind(middle, "cable", REACH, [(last, 1)])
    upper = from_behind(middle, "cable", -REACH)
    own = own_spectra(records, shared, share)
    products = far_products(starts, [*own, *shared], [lower, middle, upper], tables[2:])
    sent = lax.all_to_all(products, "pair", 0, 0)
    return place_lags(sent, rows).reshape(1, 1, 2 * LAG + 1, rows)


def solution(mesh):
    in_specs = (P("cable", "pair"), P(), P("cable", None), P("cable", None), P("cable"))
    out_specs = P("cable", "pair", None, None)
    return jax.shard_map(
        per_device, mesh=mesh, in_specs=in_specs, out_specs=out_specs, check_vma=False
    )
```

```python
import math

import jax
import jax.numpy as jnp
import ml_dtypes
import numpy as np
from jax import lax
from jax.experimental import pallas as pl
from jax.experimental.pallas import tpu as pltpu
from jax.sharding import PartitionSpec as P

LAG = 200
REACH = 2
EPSILON = 1e-05
WIDE = 256
LAG_PAD = 512
LANES = 128
OWN_LIMIT = 49
FAR_LIMIT = 44
F32 = jnp.float32
BF16 = jnp.bfloat16


def transform_tables(samples):
    length = -(-(samples + LAG) // (4 * LANES)) * 4 * LANES
    theta = 2 * np.pi * (np.arange(length // 4) + 0.5) / length
    forward = np.outer(np.arange(samples // 2) + 0.5, theta)
    weight = 2.0 / length / math.sqrt(samples)
    tables = [np.cos(forward), np.sin(forward)]
    for first in (0, 1):
        backward = np.outer(theta, np.arange(LAG_PAD // 2) * 2 + first - LAG)
        tables += [np.cos(backward) * weight, np.sin(backward) * weight]
    return [jnp.asarray(table.astype(ml_dtypes.bfloat16)) for table in tables]


def smoothing_band(row):
    taps = row.astype(BF16).astype(F32)
    band = pltpu.roll(
        jnp.broadcast_to(taps, (WIDE, row.shape[1])), 0, 1, stride=1, stride_axis=0
    ).astype(BF16)
    return band, 1.0 / jnp.sum(taps)


def normalize(parts, band, scale):
    rows, width = parts[0].shape
    outside = jnp.zeros((rows, width), F32)
    padded = [outside] + parts + [outside]
    firsts = range(0, len(parts), 2)
    smoothed = lax.dot_general(
        jnp.concatenate(
            [jnp.abs(jnp.concatenate(padded[p : p + 4], 1)).astype(BF16) for p in firsts], 0
        ),
        band,
        (((1,), (1,)), ((), ())),
        preferred_element_type=F32,
    )
    values = jnp.concatenate([jnp.concatenate(parts[p : p + 2], 1) for p in firsts], 0)
    return (values / (smoothed * scale + EPSILON)).astype(BF16)


def fold(unit, rows):
    mirror = (
        lax.broadcasted_iota(jnp.int32, (WIDE, WIDE), 0)
        + lax.broadcasted_iota(jnp.int32, (WIDE, WIDE), 1)
        == WIDE - 1
    ).astype(BF16)
    half = unit.shape[0] // 2
    mirrored = jnp.dot(unit[:half], mirror, preferred_element_type=F32)
    later = unit[half:].astype(F32)
    even, odd = [], []
    for start in range(0, half, rows):
        ahead = later[start : start + rows]
        behind = mirrored[half - start - rows : half - start]
        even.append((ahead + behind).astype(BF16))
        odd.append((ahead - behind).astype(BF16))
    even, odd = jnp.concatenate(even, 1), jnp.concatenate(odd, 1)
    sign = 1 - 2 * lax.rem(lax.broadcasted_iota(jnp.int32, even.shape, 1), 2)
    sign = sign.astype(F32).astype(BF16)
    return jnp.concatenate([even, odd * sign], 0), jnp.concatenate([odd, even * sign], 0)


def own_kernel(
    raw_ref,
    row_ref,
    cos_hbm,
    sin_hbm,
    own_cos_ref,
    own_sin_ref,
    cos_ref,
    sin_ref,
    band_ref,
    scale_ref,
    copied,
):
    pieces, rows, _ = raw_ref.shape
    copies = [
        pltpu.make_async_copy(cos_hbm, cos_ref, copied.at[0]),
        pltpu.make_async_copy(sin_hbm, sin_ref, copied.at[1]),
    ]
    for copy in copies:
        copy.start()
    band, scale = smoothing_band(row_ref[...])
    band_ref[...] = band
    scale_ref[...] = jnp.broadcast_to(scale, scale_ref.shape)
    for_cos, for_sin = fold(
        normalize([raw_ref[p].astype(F32) for p in range(pieces)], band, scale), rows
    )
    spare = own_cos_ref.shape[1] - rows
    tiles = cos_ref.shape[1] // LANES
    for copy, part, table_ref, lower_ref, upper_ref in (
        (copies[0], for_cos, cos_ref, own_cos_ref, own_sin_ref),
        (copies[1], for_sin, sin_ref, own_sin_ref, own_cos_ref),
    ):
        copy.wait()
        spectrum = jnp.dot(part, table_ref[...], preferred_element_type=F32)
        for tile in range(tiles):
            lanes = spectrum[:, tile * LANES : (tile + 1) * LANES]
            lower_ref[tile, :rows] = lanes[:rows]
            lower_ref[tile, rows:] = lanes[:spare]
            upper_ref[tiles + tile, :rows] = lanes[rows:]
            upper_ref[tiles + tile, rows:] = lanes[rows : rows + spare]


def own_spectra(records, taps_row, tables, spare):
    rows = records.shape[1]
    frequencies = 2 * tables[0].shape[1]
    vmem = pl.BlockSpec(memory_space=pltpu.VMEM)
    hbm = pl.BlockSpec(memory_space=pltpu.HBM)
    spectrum = jax.ShapeDtypeStruct((frequencies // LANES, rows + spare, LANES), F32)
    return pl.pallas_call(
        own_kernel,
        out_shape=[spectrum, spectrum]
        + [jax.ShapeDtypeStruct(table.shape, BF16) for table in tables]
        + [
            jax.ShapeDtypeStruct((WIDE, 2 * WIDE), BF16),
            jax.ShapeDtypeStruct((1, WIDE), F32),
        ],
        in_specs=[vmem, vmem, hbm, hbm],
        out_specs=[vmem] * 6,
        scratch_shapes=[pltpu.SemaphoreType.DMA((2,))],
        compiler_params=pltpu.CompilerParams(vmem_limit_bytes=OWN_LIMIT << 20),
    )(records, taps_row, *tables)


def far_kernel(
    start_any,
    own_cos_ref,
    own_sin_ref,
    cos_ref,
    sin_ref,
    band_ref,
    scale_ref,
    *refs,
):
    run_refs = refs[:3]
    back_hbms = refs[3:7]
    out_ref, far_cos_ref, far_sin_ref = refs[7:10]
    sum_refs, back_refs = refs[10:14], refs[14:18]
    start_ref, copied = refs[18:]
    start_copy = pltpu.make_async_copy(start_any, start_ref, copied.at[4])
    start_copy.start()
    copies = [
        pltpu.make_async_copy(source, target, copied.at[place])
        for place, (source, target) in enumerate(zip(back_hbms, back_refs))
    ]
    for copy in copies:
        copy.start()
    _, pieces, share, _ = run_refs[0].shape
    block_rows = share * pieces
    blocks = [(ref, place) for ref in run_refs for place in range(ref.shape[0])]
    rows = len(blocks) * share
    quarter = cos_ref.shape[1]
    frequencies = 2 * quarter
    inside = (lax.axis_size("cable") + REACH - lax.axis_index("cable")) * share
    within = lax.broadcasted_iota(jnp.int32, (rows, run_refs[0].shape[3]), 0) < inside
    parts = [
        jnp.where(
            within,
            jnp.concatenate([ref[place, p].astype(F32) for ref, place in blocks], 0),
            0.0,
        )
        for p in range(pieces)
    ]
    for_cos, for_sin = fold(normalize(parts, band_ref[...], scale_ref[...]), rows)
    spectrum = jnp.dot(for_cos, cos_ref[...], preferred_element_type=F32)
    far_cos_ref[:, :quarter] = spectrum[:rows]
    far_sin_ref[:, quarter:] = spectrum[rows:]
    spectrum = jnp.dot(for_sin, sin_ref[...], preferred_element_type=F32)
    far_sin_ref[:, :quarter] = spectrum[:rows]
    far_cos_ref[:, quarter:] = spectrum[rows:]

    slots = start_ref.shape[0]
    first = lax.axis_index("pair") * share
    place = first + lax.broadcasted_iota(jnp.int32, (share, frequencies), 0)
    pair = []
    start_copy.wait()
    for slot in range(slots):
        start = jnp.maximum(start_ref[slot], 0)
        block = lax.div(start, block_rows)
        offset = lax.rem(start, block_rows)
        lower = pl.ds(pl.multiple_of(block * share, share), share)
        upper = pl.ds(pl.multiple_of(block * share + share, share), share)
        own = pl.ds(lax.rem(first - offset + block_rows, block_rows), share)
        before = place >= offset
        far_cos = jnp.where(before, far_cos_ref[lower], far_cos_ref[upper])
        far_sin = jnp.where(before, far_sin_ref[lower], far_sin_ref[upper])
        tiles = range(frequencies // LANES)
        own_cos = jnp.concatenate([own_cos_ref[tile, own] for tile in tiles], 1)
        own_sin = jnp.concatenate([own_sin_ref[tile, own] for tile in tiles], 1)
        real = own_cos * far_cos + own_sin * far_sin
        imag = own_cos * far_sin - own_sin * far_cos
        pair.append(
            (
                real[:, :quarter] + real[:, quarter:],
                imag[:, :quarter] - imag[:, quarter:],
                real[:, :quarter] - real[:, quarter:],
                imag[:, :quarter] + imag[:, quarter:],
            )
        )
        if len(pair) * share == 16:
            begin = (slot + 1) * share - 16
            for sum_ref, values in zip(sum_refs, zip(*pair)):
                sum_ref[begin : begin + 16] = jnp.concatenate(values, 0).astype(BF16)
            pair = []
    for copy in copies:
        copy.wait()
    lag_sums = [
        jnp.dot(sum_ref[...], back_ref[...], preferred_element_type=F32)
        for sum_ref, back_ref in zip(sum_refs, back_refs)
    ]
    result = jnp.concatenate([lag_sums[0] + lag_sums[1], lag_sums[2] + lag_sums[3]], 1)
    tile = (share * LAG_PAD // LANES, LANES)
    last_lane = (lax.broadcasted_iota(jnp.int32, tile, 0) >= tile[0] - share) & (
        lax.broadcasted_iota(jnp.int32, tile, 1) == LANES - 1
    )
    for slot in range(slots):
        lags = jnp.concatenate(
            [
                result[slot * share : (slot + 1) * share, lane : lane + LANES]
                for lane in range(0, LAG_PAD, LANES)
            ],
            0,
        )
        start = start_ref[slot]
        offset = lax.rem(jnp.maximum(start, 0), block_rows).astype(F32)
        lags = jnp.where(start >= 0, lags, 0.0)
        out_ref[slot] = jnp.where(last_lane, offset, lags).astype(BF16)


def far_products(starts, own, runs, tables):
    share = runs[0].shape[2]
    slots = starts.shape[0]
    rows = sum(run.shape[0] for run in runs) * share
    quarter = own[2].shape[1]
    frequencies = 2 * quarter
    vmem = pl.BlockSpec(memory_space=pltpu.VMEM)
    hbm = pl.BlockSpec(memory_space=pltpu.HBM)
    anywhere = pl.BlockSpec(memory_space=pl.ANY)
    return pl.pallas_call(
        far_kernel,
        out_shape=jax.ShapeDtypeStruct((slots, share * LAG_PAD // LANES, LANES), BF16),
        in_specs=[anywhere] + [vmem] * (len(own) + len(runs)) + [hbm] * 4,
        out_specs=vmem,
        scratch_shapes=[
            pltpu.VMEM((rows, frequencies), F32),
            pltpu.VMEM((rows, frequencies), F32),
        ]
        + [pltpu.VMEM((slots * share, quarter), BF16)] * 4
        + [pltpu.VMEM(table.shape, BF16) for table in tables]
        + [
            pltpu.SMEM((slots,), jnp.int32),
            pltpu.SemaphoreType.DMA((5,)),
        ],
        compiler_params=pltpu.CompilerParams(vmem_limit_bytes=FAR_LIMIT << 20),
    )(starts, *own, *runs, *tables)


def place_kernel(sent_ref, out_hbm, out_ref, copied):
    senders, rows, lanes = sent_ref.shape
    tiles = LAG_PAD // lanes
    share = rows // tiles
    values = [sent_ref[sender].astype(F32) for sender in range(senders)]
    lags = [
        jnp.concatenate([value[step * share : (step + 1) * share] for value in values], 0)
        for step in range(tiles)
    ]
    block_rows = senders * share
    row = lax.broadcasted_iota(jnp.int32, (block_rows, block_rows), 0)
    channel = lax.broadcasted_iota(jnp.int32, (block_rows, block_rows), 1)
    offset = lags[-1][:, lanes - 1 :].astype(jnp.int32)
    ahead = row - offset - channel
    turn = ((ahead == 0) | (ahead == -block_rows)).astype(BF16)
    total = out_ref.shape[0]
    written = []
    for step in range(tiles // 2):
        begin, stop = 2 * step * lanes, min(total, 2 * (step + 1) * lanes)
        for odd in (0, 1):
            count = (stop - begin + 1 - odd) // 2
            out_ref[pl.ds(begin + odd, count, stride=2)] = lax.dot_general(
                lags[step + odd * tiles // 2].astype(BF16),
                turn,
                (((0,), (0,)), ((), ())),
                preferred_element_type=F32,
            )[:count]
        span = pl.ds(begin, stop - begin)
        written.append(
            pltpu.make_async_copy(out_ref.at[span], out_hbm.at[span, 0], copied.at[step])
        )
        written[-1].start()
    for copy in written:
        copy.wait()


def place_lags(sent, rows):
    vmem = pl.BlockSpec(memory_space=pltpu.VMEM)
    hbm = pl.BlockSpec(memory_space=pltpu.HBM)
    return pl.pallas_call(
        place_kernel,
        out_shape=jax.ShapeDtypeStruct((2 * LAG + 1, 1, rows), F32),
        in_specs=[vmem],
        out_specs=hbm,
        scratch_shapes=[
            pltpu.VMEM((2 * LAG + 1, rows), F32),
            pltpu.SemaphoreType.DMA((LAG_PAD // LANES // 2,)),
        ],
        compiler_params=pltpu.CompilerParams(vmem_limit_bytes=8 << 20),
    )(sent)


def from_behind(value, axis, steps, also=()):
    count = lax.axis_size(axis)
    first, last = (max(0, -steps), min(count, count - steps))
    pairs = [(source, source + steps) for source in range(first, last)]
    return lax.ppermute(value, axis, pairs + list(also))


def per_device(raw_strain, smooth_taps, partner_block, chan_offset, pair_count):
    rows = raw_strain.shape[0]
    share = rows // lax.axis_size("pair")
    first_block = lax.axis_index("cable") - REACH
    records = lax.all_gather(raw_strain, "pair", axis=0)
    mine = lax.dynamic_slice_in_dim(records, lax.axis_index("pair") * share, share, 1)
    tables = transform_tables(records.shape[0] * records.shape[2])
    mine, smooth_taps, partner_block, chan_offset, pair_count = lax.optimization_barrier(
        (mine, smooth_taps, partner_block, chan_offset, pair_count)
    )
    last = lax.axis_size("cable") - 1
    middle = jnp.stack([mine, from_behind(mine, "cable", -1, [(0, last)])], 0)
    starts = (partner_block[0] - first_block) * rows + chan_offset[0]
    live = jnp.arange(starts.shape[0], dtype=jnp.int32) < pair_count
    starts = jnp.where(live, starts, -1)
    lead = records.shape[2] - (smooth_taps.shape[0] - 1) // 2
    taps_row = jnp.pad(smooth_taps, (lead, 2 * WIDE - lead - smooth_taps.shape[0]))[None]
    middle, starts, taps_row = lax.optimization_barrier((middle, starts, taps_row))
    lower = from_behind(middle, "cable", REACH, [(last, 1)])
    upper = from_behind(middle, "cable", -REACH)
    own = own_spectra(records, taps_row, tables[:2], share)
    products = far_products(starts, own, [lower, middle, upper], tables[2:])
    sent = lax.all_to_all(products, "pair", 0, 0)
    return place_lags(sent, rows).reshape(1, 1, 2 * LAG + 1, rows)


def solution(mesh):
    in_specs = (P("cable", "pair"), P(), P("cable", None), P("cable", None), P("cable"))
    out_specs = P("cable", "pair", None, None)
    return jax.shard_map(
        per_device, mesh=mesh, in_specs=in_specs, out_specs=out_specs, check_vma=False
    )
```

```python
import math

import jax
import jax.numpy as jnp
import ml_dtypes
import numpy as np
from jax import lax
from jax.experimental import pallas as pl
from jax.experimental.pallas import tpu as pltpu
from jax.sharding import PartitionSpec as P

LAG = 200
REACH = 2
EPSILON = 1e-05
WIDE = 256
LAG_PAD = 512
LANES = 128
OWN_LIMIT = 49
FAR_LIMIT = 44
F32 = jnp.float32
BF16 = jnp.bfloat16


def transform_tables(samples):
    length = -(-(samples + LAG) // (4 * LANES)) * 4 * LANES
    theta = 2 * np.pi * (np.arange(length // 4) + 0.5) / length
    forward = np.outer(np.arange(samples // 2) + 0.5, theta)
    weight = 2.0 / length / math.sqrt(samples)
    tables = [np.cos(forward), np.sin(forward)]
    for first in (0, 1):
        backward = np.outer(theta, np.arange(LAG_PAD // 2) * 2 + first - LAG)
        tables += [np.cos(backward) * weight, np.sin(backward) * weight]
    return [jnp.asarray(table.astype(ml_dtypes.bfloat16)) for table in tables]


def smoothing_band(row):
    taps = row.astype(BF16).astype(F32)
    band = pltpu.roll(
        jnp.broadcast_to(taps, (WIDE, row.shape[1])), 0, 1, stride=1, stride_axis=0
    ).astype(BF16)
    return band, 1.0 / jnp.sum(taps)


def normalize(parts, band, scale):
    rows, width = parts[0].shape
    outside = jnp.zeros((rows, width), F32)
    padded = [outside] + parts + [outside]
    firsts = range(0, len(parts), 2)
    smoothed = lax.dot_general(
        jnp.concatenate(
            [jnp.abs(jnp.concatenate(padded[p : p + 4], 1)).astype(BF16) for p in firsts], 0
        ),
        band,
        (((1,), (1,)), ((), ())),
        preferred_element_type=F32,
    )
    values = jnp.concatenate([jnp.concatenate(parts[p : p + 2], 1) for p in firsts], 0)
    return (values / (smoothed * scale + EPSILON)).astype(BF16)


def fold(unit, rows):
    mirror = (
        lax.broadcasted_iota(jnp.int32, (WIDE, WIDE), 0)
        + lax.broadcasted_iota(jnp.int32, (WIDE, WIDE), 1)
        == WIDE - 1
    ).astype(BF16)
    half = unit.shape[0] // 2
    mirrored = jnp.dot(unit[:half], mirror, preferred_element_type=F32)
    later = unit[half:].astype(F32)
    even, odd = [], []
    for start in range(0, half, rows):
        ahead = later[start : start + rows]
        behind = mirrored[half - start - rows : half - start]
        even.append((ahead + behind).astype(BF16))
        odd.append((ahead - behind).astype(BF16))
    even, odd = jnp.concatenate(even, 1), jnp.concatenate(odd, 1)
    sign = 1 - 2 * lax.rem(lax.broadcasted_iota(jnp.int32, even.shape, 1), 2)
    sign = sign.astype(F32).astype(BF16)
    return jnp.concatenate([even, odd * sign], 0), jnp.concatenate([odd, even * sign], 0)


def own_kernel(
    raw_ref,
    row_ref,
    cos_hbm,
    sin_hbm,
    own_cos_ref,
    own_sin_ref,
    cos_ref,
    sin_ref,
    band_ref,
    scale_ref,
    copied,
):
    pieces, rows, _ = raw_ref.shape
    copies = [
        pltpu.make_async_copy(cos_hbm, cos_ref, copied.at[0]),
        pltpu.make_async_copy(sin_hbm, sin_ref, copied.at[1]),
    ]
    for copy in copies:
        copy.start()
    band, scale = smoothing_band(row_ref[...])
    band_ref[...] = band
    scale_ref[...] = jnp.broadcast_to(scale, scale_ref.shape)
    for_cos, for_sin = fold(
        normalize([raw_ref[p].astype(F32) for p in range(pieces)], band, scale), rows
    )
    spare = own_cos_ref.shape[1] - rows
    tiles = cos_ref.shape[1] // LANES
    for copy, part, table_ref, lower_ref, upper_ref in (
        (copies[0], for_cos, cos_ref, own_cos_ref, own_sin_ref),
        (copies[1], for_sin, sin_ref, own_sin_ref, own_cos_ref),
    ):
        copy.wait()
        spectrum = jnp.dot(part, table_ref[...], preferred_element_type=F32)
        for tile in range(tiles):
            lanes = spectrum[:, tile * LANES : (tile + 1) * LANES]
            lower_ref[tile, :rows] = lanes[:rows]
            lower_ref[tile, rows:] = lanes[:spare]
            upper_ref[tiles + tile, :rows] = lanes[rows:]
            upper_ref[tiles + tile, rows:] = lanes[rows : rows + spare]


def own_spectra(records, taps_row, tables, spare):
    rows = records.shape[1]
    frequencies = 2 * tables[0].shape[1]
    vmem = pl.BlockSpec(memory_space=pltpu.VMEM)
    hbm = pl.BlockSpec(memory_space=pltpu.HBM)
    spectrum = jax.ShapeDtypeStruct((frequencies // LANES, rows + spare, LANES), F32)
    return pl.pallas_call(
        own_kernel,
        out_shape=[spectrum, spectrum]
        + [jax.ShapeDtypeStruct(table.shape, BF16) for table in tables]
        + [
            jax.ShapeDtypeStruct((WIDE, 2 * WIDE), BF16),
            jax.ShapeDtypeStruct((1, WIDE), F32),
        ],
        in_specs=[vmem, vmem, hbm, hbm],
        out_specs=[vmem] * 6,
        scratch_shapes=[pltpu.SemaphoreType.DMA((2,))],
        compiler_params=pltpu.CompilerParams(vmem_limit_bytes=OWN_LIMIT << 20),
    )(records, taps_row, *tables)


def far_kernel(
    block_any,
    offset_any,
    count_ref,
    own_cos_ref,
    own_sin_ref,
    cos_ref,
    sin_ref,
    band_ref,
    scale_ref,
    *refs,
):
    run_refs = refs[:3]
    back_hbms = refs[3:7]
    out_ref, far_cos_ref, far_sin_ref = refs[7:10]
    sum_refs, back_refs = refs[10:14], refs[14:18]
    block_ref, offset_ref, copied = refs[18:]
    slot_copies = [
        pltpu.make_async_copy(block_any, block_ref, copied.at[4]),
        pltpu.make_async_copy(offset_any, offset_ref, copied.at[5]),
    ]
    for copy in slot_copies:
        copy.start()
    copies = [
        pltpu.make_async_copy(source, target, copied.at[place])
        for place, (source, target) in enumerate(zip(back_hbms, back_refs))
    ]
    for copy in copies:
        copy.start()
    _, pieces, share, _ = run_refs[0].shape
    block_rows = share * pieces
    blocks = [(ref, place) for ref in run_refs for place in range(ref.shape[0])]
    rows = len(blocks) * share
    quarter = cos_ref.shape[1]
    frequencies = 2 * quarter
    inside = (lax.axis_size("cable") + REACH - lax.axis_index("cable")) * share
    within = lax.broadcasted_iota(jnp.int32, (rows, run_refs[0].shape[3]), 0) < inside
    parts = [
        jnp.where(
            within,
            jnp.concatenate([ref[place, p].astype(F32) for ref, place in blocks], 0),
            0.0,
        )
        for p in range(pieces)
    ]
    for_cos, for_sin = fold(normalize(parts, band_ref[...], scale_ref[...]), rows)
    spectrum = jnp.dot(for_cos, cos_ref[...], preferred_element_type=F32)
    far_cos_ref[:, :quarter] = spectrum[:rows]
    far_sin_ref[:, quarter:] = spectrum[rows:]
    spectrum = jnp.dot(for_sin, sin_ref[...], preferred_element_type=F32)
    far_sin_ref[:, :quarter] = spectrum[:rows]
    far_cos_ref[:, quarter:] = spectrum[rows:]

    slots = block_ref.shape[1]
    first_block = lax.axis_index("cable") - REACH
    first = lax.axis_index("pair") * share
    place = first + lax.broadcasted_iota(jnp.int32, (share, frequencies), 0)
    pair = []
    for copy in slot_copies:
        copy.wait()
    for slot in range(slots):
        block = block_ref[0, slot] - first_block
        offset = offset_ref[0, slot]
        lower = pl.ds(pl.multiple_of(block * share, share), share)
        upper = pl.ds(pl.multiple_of(block * share + share, share), share)
        own = pl.ds(lax.rem(first - offset + block_rows, block_rows), share)
        before = place >= offset
        far_cos = jnp.where(before, far_cos_ref[lower], far_cos_ref[upper])
        far_sin = jnp.where(before, far_sin_ref[lower], far_sin_ref[upper])
        tiles = range(frequencies // LANES)
        own_cos = jnp.concatenate([own_cos_ref[tile, own] for tile in tiles], 1)
        own_sin = jnp.concatenate([own_sin_ref[tile, own] for tile in tiles], 1)
        real = own_cos * far_cos + own_sin * far_sin
        imag = own_cos * far_sin - own_sin * far_cos
        pair.append(
            (
                real[:, :quarter] + real[:, quarter:],
                imag[:, :quarter] - imag[:, quarter:],
                real[:, :quarter] - real[:, quarter:],
                imag[:, :quarter] + imag[:, quarter:],
            )
        )
        if len(pair) * share == 16:
            begin = (slot + 1) * share - 16
            for sum_ref, values in zip(sum_refs, zip(*pair)):
                sum_ref[begin : begin + 16] = jnp.concatenate(values, 0).astype(BF16)
            pair = []
    for copy in copies:
        copy.wait()
    lag_sums = [
        jnp.dot(sum_ref[...], back_ref[...], preferred_element_type=F32)
        for sum_ref, back_ref in zip(sum_refs, back_refs)
    ]
    result = jnp.concatenate([lag_sums[0] + lag_sums[1], lag_sums[2] + lag_sums[3]], 1)
    tile = (share * LAG_PAD // LANES, LANES)
    last_lane = (lax.broadcasted_iota(jnp.int32, tile, 0) >= tile[0] - share) & (
        lax.broadcasted_iota(jnp.int32, tile, 1) == LANES - 1
    )
    count = jnp.broadcast_to(count_ref[...], tile)
    for slot in range(slots):
        lags = jnp.concatenate(
            [
                result[slot * share : (slot + 1) * share, lane : lane + LANES]
                for lane in range(0, LAG_PAD, LANES)
            ],
            0,
        )
        offset = offset_ref[0, slot].astype(F32)
        lags = jnp.where(slot < count, lags, 0.0)
        out_ref[slot] = jnp.where(last_lane, offset, lags).astype(BF16)


def far_products(slot_tables, own, runs, tables):
    share = runs[0].shape[2]
    slots = slot_tables[0].shape[1]
    rows = sum(run.shape[0] for run in runs) * share
    quarter = own[2].shape[1]
    frequencies = 2 * quarter
    vmem = pl.BlockSpec(memory_space=pltpu.VMEM)
    hbm = pl.BlockSpec(memory_space=pltpu.HBM)
    anywhere = pl.BlockSpec(memory_space=pl.ANY)
    return pl.pallas_call(
        far_kernel,
        out_shape=jax.ShapeDtypeStruct((slots, share * LAG_PAD // LANES, LANES), BF16),
        in_specs=[anywhere] * 2 + [vmem] * (1 + len(own) + len(runs)) + [hbm] * 4,
        out_specs=vmem,
        scratch_shapes=[
            pltpu.VMEM((rows, frequencies), F32),
            pltpu.VMEM((rows, frequencies), F32),
        ]
        + [pltpu.VMEM((slots * share, quarter), BF16)] * 4
        + [pltpu.VMEM(table.shape, BF16) for table in tables]
        + [
            pltpu.SMEM((1, slots), jnp.int32),
            pltpu.SMEM((1, slots), jnp.int32),
            pltpu.SemaphoreType.DMA((6,)),
        ],
        compiler_params=pltpu.CompilerParams(vmem_limit_bytes=FAR_LIMIT << 20),
    )(*slot_tables, *own, *runs, *tables)


def place_kernel(sent_ref, out_hbm, out_ref, copied):
    senders, rows, lanes = sent_ref.shape
    tiles = LAG_PAD // lanes
    share = rows // tiles
    values = [sent_ref[sender].astype(F32) for sender in range(senders)]
    lags = [
        jnp.concatenate([value[step * share : (step + 1) * share] for value in values], 0)
        for step in range(tiles)
    ]
    block_rows = senders * share
    row = lax.broadcasted_iota(jnp.int32, (block_rows, block_rows), 0)
    channel = lax.broadcasted_iota(jnp.int32, (block_rows, block_rows), 1)
    offset = lags[-1][:, lanes - 1 :].astype(jnp.int32)
    ahead = row - offset - channel
    turn = ((ahead == 0) | (ahead == -block_rows)).astype(BF16)
    total = out_ref.shape[0]
    written = []
    for step in range(tiles // 2):
        begin, stop = 2 * step * lanes, min(total, 2 * (step + 1) * lanes)
        for odd in (0, 1):
            count = (stop - begin + 1 - odd) // 2
            out_ref[pl.ds(begin + odd, count, stride=2)] = lax.dot_general(
                lags[step + odd * tiles // 2].astype(BF16),
                turn,
                (((0,), (0,)), ((), ())),
                preferred_element_type=F32,
            )[:count]
        span = pl.ds(begin, stop - begin)
        written.append(
            pltpu.make_async_copy(out_ref.at[span], out_hbm.at[span, 0], copied.at[step])
        )
        written[-1].start()
    for copy in written:
        copy.wait()


def place_lags(sent, rows):
    vmem = pl.BlockSpec(memory_space=pltpu.VMEM)
    hbm = pl.BlockSpec(memory_space=pltpu.HBM)
    return pl.pallas_call(
        place_kernel,
        out_shape=jax.ShapeDtypeStruct((2 * LAG + 1, 1, rows), F32),
        in_specs=[vmem],
        out_specs=hbm,
        scratch_shapes=[
            pltpu.VMEM((2 * LAG + 1, rows), F32),
            pltpu.SemaphoreType.DMA((LAG_PAD // LANES // 2,)),
        ],
        compiler_params=pltpu.CompilerParams(vmem_limit_bytes=8 << 20),
    )(sent)


def from_behind(value, axis, steps, also=()):
    count = lax.axis_size(axis)
    first, last = (max(0, -steps), min(count, count - steps))
    pairs = [(source, source + steps) for source in range(first, last)]
    return lax.ppermute(value, axis, pairs + list(also))


def per_device(raw_strain, smooth_taps, partner_block, chan_offset, pair_count):
    rows = raw_strain.shape[0]
    share = rows // lax.axis_size("pair")
    records = lax.all_gather(raw_strain, "pair", axis=0)
    mine = lax.dynamic_slice_in_dim(records, lax.axis_index("pair") * share, share, 1)
    tables = transform_tables(records.shape[0] * records.shape[2])
    mine, smooth_taps, pair_count = lax.optimization_barrier((mine, smooth_taps, pair_count))
    lead = records.shape[2] - (smooth_taps.shape[0] - 1) // 2
    taps_row = jnp.pad(smooth_taps, (lead, 2 * WIDE - lead - smooth_taps.shape[0]))[None]
    last = lax.axis_size("cable") - 1
    middle = jnp.stack([mine, from_behind(mine, "cable", -1, [(0, last)])], 0)
    middle, records, taps_row, count = lax.optimization_barrier(
        (middle, records, taps_row, pair_count[None])
    )
    lower = from_behind(middle, "cable", REACH, [(last, 1)])
    upper = from_behind(middle, "cable", -REACH)
    own = own_spectra(records, taps_row, tables[:2], share)
    slot_tables = (partner_block, chan_offset, count)
    products = far_products(slot_tables, own, [lower, middle, upper], tables[2:])
    sent = lax.all_to_all(products, "pair", 0, 0)
    return place_lags(sent, rows).reshape(1, 1, 2 * LAG + 1, rows)


def solution(mesh):
    in_specs = (P("cable", "pair"), P(), P("cable", None), P("cable", None), P("cable"))
    out_specs = P("cable", "pair", None, None)
    return jax.shard_map(
        per_device, mesh=mesh, in_specs=in_specs, out_specs=out_specs, check_vma=False
    )
```

```python
import math

import jax
import jax.numpy as jnp
import ml_dtypes
import numpy as np
from jax import lax
from jax.experimental import pallas as pl
from jax.experimental.pallas import tpu as pltpu
from jax.sharding import PartitionSpec as P

LAG = 200
REACH = 2
EPSILON = 1e-05
WIDE = 256
LAG_PAD = 512
LANES = 128
OWN_LIMIT = 49
FAR_LIMIT = 44
F32 = jnp.float32
BF16 = jnp.bfloat16


def transform_tables(samples):
    length = -(-(samples + LAG) // (4 * LANES)) * 4 * LANES
    theta = 2 * np.pi * (np.arange(length // 4) + 0.5) / length
    forward = np.outer(np.arange(samples // 2) + 0.5, theta)
    weight = 2.0 / length / math.sqrt(samples)
    tables = [np.cos(forward), np.sin(forward)]
    for first in (0, 1):
        backward = np.outer(theta, np.arange(LAG_PAD // 2) * 2 + first - LAG)
        tables += [np.cos(backward) * weight, np.sin(backward) * weight]
    return [jnp.asarray(table.astype(ml_dtypes.bfloat16)) for table in tables]


def smoothing_band(row):
    taps = row.astype(BF16).astype(F32)
    band = pltpu.roll(
        jnp.broadcast_to(taps, (WIDE, row.shape[1])), 0, 1, stride=1, stride_axis=0
    ).astype(BF16)
    return band, 1.0 / jnp.sum(taps)


def normalize(parts, band, scale):
    rows, width = parts[0].shape
    outside = jnp.zeros((rows, width), F32)
    padded = [outside] + parts + [outside]
    firsts = range(0, len(parts), 2)
    smoothed = lax.dot_general(
        jnp.concatenate(
            [jnp.abs(jnp.concatenate(padded[p : p + 4], 1)).astype(BF16) for p in firsts], 0
        ),
        band,
        (((1,), (1,)), ((), ())),
        preferred_element_type=F32,
    )
    values = jnp.concatenate([jnp.concatenate(parts[p : p + 2], 1) for p in firsts], 0)
    return (values / (smoothed * scale + EPSILON)).astype(BF16)


def fold(unit, rows):
    mirror = (
        lax.broadcasted_iota(jnp.int32, (WIDE, WIDE), 0)
        + lax.broadcasted_iota(jnp.int32, (WIDE, WIDE), 1)
        == WIDE - 1
    ).astype(BF16)
    half = unit.shape[0] // 2
    mirrored = jnp.dot(unit[:half], mirror, preferred_element_type=F32)
    later = unit[half:].astype(F32)
    even, odd = [], []
    for start in range(0, half, rows):
        ahead = later[start : start + rows]
        behind = mirrored[half - start - rows : half - start]
        even.append((ahead + behind).astype(BF16))
        odd.append((ahead - behind).astype(BF16))
    even, odd = jnp.concatenate(even, 1), jnp.concatenate(odd, 1)
    sign = 1 - 2 * lax.rem(lax.broadcasted_iota(jnp.int32, even.shape, 1), 2)
    sign = sign.astype(F32).astype(BF16)
    return jnp.concatenate([even, odd * sign], 0), jnp.concatenate([odd, even * sign], 0)


def own_kernel(
    raw_ref,
    row_ref,
    cos_hbm,
    sin_hbm,
    own_cos_ref,
    own_sin_ref,
    cos_ref,
    sin_ref,
    band_ref,
    scale_ref,
    copied,
):
    pieces, rows, _ = raw_ref.shape
    copies = [
        pltpu.make_async_copy(cos_hbm, cos_ref, copied.at[0]),
        pltpu.make_async_copy(sin_hbm, sin_ref, copied.at[1]),
    ]
    for copy in copies:
        copy.start()
    band, scale = smoothing_band(row_ref[...])
    band_ref[...] = band
    scale_ref[...] = jnp.broadcast_to(scale, scale_ref.shape)
    for_cos, for_sin = fold(
        normalize([raw_ref[p].astype(F32) for p in range(pieces)], band, scale), rows
    )
    spare = own_cos_ref.shape[1] - rows
    tiles = cos_ref.shape[1] // LANES
    for copy, part, table_ref, lower_ref, upper_ref in (
        (copies[0], for_cos, cos_ref, own_cos_ref, own_sin_ref),
        (copies[1], for_sin, sin_ref, own_sin_ref, own_cos_ref),
    ):
        copy.wait()
        spectrum = jnp.dot(part, table_ref[...], preferred_element_type=F32)
        for tile in range(tiles):
            lanes = spectrum[:, tile * LANES : (tile + 1) * LANES]
            lower_ref[tile, :rows] = lanes[:rows]
            lower_ref[tile, rows:] = lanes[:spare]
            upper_ref[tiles + tile, :rows] = lanes[rows:]
            upper_ref[tiles + tile, rows:] = lanes[rows : rows + spare]


def own_spectra(records, taps_row, tables, spare):
    rows = records.shape[1]
    frequencies = 2 * tables[0].shape[1]
    vmem = pl.BlockSpec(memory_space=pltpu.VMEM)
    hbm = pl.BlockSpec(memory_space=pltpu.HBM)
    spectrum = jax.ShapeDtypeStruct((frequencies // LANES, rows + spare, LANES), F32)
    return pl.pallas_call(
        own_kernel,
        out_shape=[spectrum, spectrum]
        + [jax.ShapeDtypeStruct(table.shape, BF16) for table in tables]
        + [
            jax.ShapeDtypeStruct((WIDE, 2 * WIDE), BF16),
            jax.ShapeDtypeStruct((1, WIDE), F32),
        ],
        in_specs=[vmem, vmem, hbm, hbm],
        out_specs=[vmem] * 6,
        scratch_shapes=[pltpu.SemaphoreType.DMA((2,))],
        compiler_params=pltpu.CompilerParams(vmem_limit_bytes=OWN_LIMIT << 20),
    )(records, taps_row, *tables)


def far_kernel(
    start_any,
    own_cos_ref,
    own_sin_ref,
    cos_ref,
    sin_ref,
    band_ref,
    scale_ref,
    *refs,
):
    run_refs = refs[:3]
    back_hbms = refs[3:7]
    out_ref, far_cos_ref, far_sin_ref = refs[7:10]
    sum_refs, back_refs = refs[10:14], refs[14:18]
    start_ref, copied = refs[18:]
    start_copy = pltpu.make_async_copy(start_any, start_ref, copied.at[4])
    start_copy.start()
    copies = [
        pltpu.make_async_copy(source, target, copied.at[place])
        for place, (source, target) in enumerate(zip(back_hbms, back_refs))
    ]
    for copy in copies:
        copy.start()
    _, pieces, share, _ = run_refs[0].shape
    block_rows = share * pieces
    blocks = [(ref, place) for ref in run_refs for place in range(ref.shape[0])]
    rows = len(blocks) * share
    quarter = cos_ref.shape[1]
    frequencies = 2 * quarter
    cable = lax.axis_index("cable")
    reverse = lax.rem(lax.div(cable, REACH), 2) == 1

    def stands(block):
        return jnp.where(reverse, 2 * REACH - block + 2 * lax.rem(block, REACH), block)

    run_row = lax.broadcasted_iota(jnp.int32, (rows, run_refs[0].shape[3]), 0)
    within = stands(lax.div(run_row, share)) < lax.axis_size("cable") + REACH - cable
    parts = [
        jnp.where(
            within,
            jnp.concatenate([ref[place, p].astype(F32) for ref, place in blocks], 0),
            0.0,
        )
        for p in range(pieces)
    ]
    for_cos, for_sin = fold(normalize(parts, band_ref[...], scale_ref[...]), rows)
    spectrum = jnp.dot(for_cos, cos_ref[...], preferred_element_type=F32)
    far_cos_ref[:, :quarter] = spectrum[:rows]
    far_sin_ref[:, quarter:] = spectrum[rows:]
    spectrum = jnp.dot(for_sin, sin_ref[...], preferred_element_type=F32)
    far_sin_ref[:, :quarter] = spectrum[:rows]
    far_cos_ref[:, quarter:] = spectrum[rows:]

    slots = start_ref.shape[0]
    first = lax.axis_index("pair") * share
    place = first + lax.broadcasted_iota(jnp.int32, (share, frequencies), 0)
    pair = []
    start_copy.wait()
    for slot in range(slots):
        start = jnp.maximum(start_ref[slot], 0)
        block = lax.div(start, block_rows)
        offset = lax.rem(start, block_rows)
        lower = pl.ds(pl.multiple_of(stands(block) * share, share), share)
        upper = pl.ds(pl.multiple_of(stands(block + 1) * share, share), share)
        own = pl.ds(lax.rem(first - offset + block_rows, block_rows), share)
        before = place >= offset
        far_cos = jnp.where(before, far_cos_ref[lower], far_cos_ref[upper])
        far_sin = jnp.where(before, far_sin_ref[lower], far_sin_ref[upper])
        tiles = range(frequencies // LANES)
        own_cos = jnp.concatenate([own_cos_ref[tile, own] for tile in tiles], 1)
        own_sin = jnp.concatenate([own_sin_ref[tile, own] for tile in tiles], 1)
        real = own_cos * far_cos + own_sin * far_sin
        imag = own_cos * far_sin - own_sin * far_cos
        pair.append(
            (
                real[:, :quarter] + real[:, quarter:],
                imag[:, :quarter] - imag[:, quarter:],
                real[:, :quarter] - real[:, quarter:],
                imag[:, :quarter] + imag[:, quarter:],
            )
        )
        if len(pair) * share == 16:
            begin = (slot + 1) * share - 16
            for sum_ref, values in zip(sum_refs, zip(*pair)):
                sum_ref[begin : begin + 16] = jnp.concatenate(values, 0).astype(BF16)
            pair = []
    for copy in copies:
        copy.wait()
    lag_sums = [
        jnp.dot(sum_ref[...], back_ref[...], preferred_element_type=F32)
        for sum_ref, back_ref in zip(sum_refs, back_refs)
    ]
    result = jnp.concatenate([lag_sums[0] + lag_sums[1], lag_sums[2] + lag_sums[3]], 1)
    tile = (share * LAG_PAD // LANES, LANES)
    last_lane = (lax.broadcasted_iota(jnp.int32, tile, 0) >= tile[0] - share) & (
        lax.broadcasted_iota(jnp.int32, tile, 1) == LANES - 1
    )
    for slot in range(slots):
        lags = jnp.concatenate(
            [
                result[slot * share : (slot + 1) * share, lane : lane + LANES]
                for lane in range(0, LAG_PAD, LANES)
            ],
            0,
        )
        start = start_ref[slot]
        offset = lax.rem(jnp.maximum(start, 0), block_rows).astype(F32)
        lags = jnp.where(start >= 0, lags, 0.0)
        out_ref[slot] = jnp.where(last_lane, offset, lags).astype(BF16)


def far_products(starts, own, runs, tables):
    share = runs[0].shape[2]
    slots = starts.shape[0]
    rows = sum(run.shape[0] for run in runs) * share
    quarter = own[2].shape[1]
    frequencies = 2 * quarter
    vmem = pl.BlockSpec(memory_space=pltpu.VMEM)
    hbm = pl.BlockSpec(memory_space=pltpu.HBM)
    anywhere = pl.BlockSpec(memory_space=pl.ANY)
    return pl.pallas_call(
        far_kernel,
        out_shape=jax.ShapeDtypeStruct((slots, share * LAG_PAD // LANES, LANES), BF16),
        in_specs=[anywhere] + [vmem] * (len(own) + len(runs)) + [hbm] * 4,
        out_specs=vmem,
        scratch_shapes=[
            pltpu.VMEM((rows, frequencies), F32),
            pltpu.VMEM((rows, frequencies), F32),
        ]
        + [pltpu.VMEM((slots * share, quarter), BF16)] * 4
        + [pltpu.VMEM(table.shape, BF16) for table in tables]
        + [
            pltpu.SMEM((slots,), jnp.int32),
            pltpu.SemaphoreType.DMA((5,)),
        ],
        compiler_params=pltpu.CompilerParams(vmem_limit_bytes=FAR_LIMIT << 20),
    )(starts, *own, *runs, *tables)


def place_kernel(sent_ref, out_hbm, out_ref, copied):
    senders, rows, lanes = sent_ref.shape
    tiles = LAG_PAD // lanes
    share = rows // tiles
    values = [sent_ref[sender].astype(F32) for sender in range(senders)]
    lags = [
        jnp.concatenate([value[step * share : (step + 1) * share] for value in values], 0)
        for step in range(tiles)
    ]
    block_rows = senders * share
    row = lax.broadcasted_iota(jnp.int32, (block_rows, block_rows), 0)
    channel = lax.broadcasted_iota(jnp.int32, (block_rows, block_rows), 1)
    offset = lags[-1][:, lanes - 1 :].astype(jnp.int32)
    ahead = row - offset - channel
    turn = ((ahead == 0) | (ahead == -block_rows)).astype(BF16)
    total = out_ref.shape[0]
    written = []
    for step in range(tiles // 2):
        begin, stop = 2 * step * lanes, min(total, 2 * (step + 1) * lanes)
        for odd in (0, 1):
            count = (stop - begin + 1 - odd) // 2
            out_ref[pl.ds(begin + odd, count, stride=2)] = lax.dot_general(
                lags[step + odd * tiles // 2].astype(BF16),
                turn,
                (((0,), (0,)), ((), ())),
                preferred_element_type=F32,
            )[:count]
        span = pl.ds(begin, stop - begin)
        written.append(
            pltpu.make_async_copy(out_ref.at[span], out_hbm.at[span, 0], copied.at[step])
        )
        written[-1].start()
    for copy in written:
        copy.wait()


def place_lags(sent, rows):
    vmem = pl.BlockSpec(memory_space=pltpu.VMEM)
    hbm = pl.BlockSpec(memory_space=pltpu.HBM)
    return pl.pallas_call(
        place_kernel,
        out_shape=jax.ShapeDtypeStruct((2 * LAG + 1, 1, rows), F32),
        in_specs=[vmem],
        out_specs=hbm,
        scratch_shapes=[
            pltpu.VMEM((2 * LAG + 1, rows), F32),
            pltpu.SemaphoreType.DMA((LAG_PAD // LANES // 2,)),
        ],
        compiler_params=pltpu.CompilerParams(vmem_limit_bytes=8 << 20),
    )(sent)


def from_behind(value, axis, steps, also=()):
    count = lax.axis_size(axis)
    first, last = (max(0, -steps), min(count, count - steps))
    pairs = [(source, source + steps) for source in range(first, last)]
    return lax.ppermute(value, axis, pairs + list(also))


def swapped(value, axis, steps, which, also=()):
    count = lax.axis_size(axis)
    firsts = [p for p in range(count - steps) if p // steps % 2 == which]
    pairs = [(p, p + steps) for p in firsts] + [(p + steps, p) for p in firsts]
    return lax.ppermute(value, axis, pairs + list(also))


def per_device(raw_strain, smooth_taps, partner_block, chan_offset, pair_count):
    rows = raw_strain.shape[0]
    share = rows // lax.axis_size("pair")
    first_block = lax.axis_index("cable") - REACH
    records = lax.all_gather(raw_strain, "pair", axis=0)
    mine = lax.dynamic_slice_in_dim(records, lax.axis_index("pair") * share, share, 1)
    tables = transform_tables(records.shape[0] * records.shape[2])
    mine, smooth_taps, partner_block, chan_offset, pair_count = lax.optimization_barrier(
        (mine, smooth_taps, partner_block, chan_offset, pair_count)
    )
    last = lax.axis_size("cable") - 1
    middle = jnp.stack([mine, from_behind(mine, "cable", -1, [(0, last)])], 0)
    starts = (partner_block[0] - first_block) * rows + chan_offset[0]
    live = jnp.arange(starts.shape[0], dtype=jnp.int32) < pair_count
    starts = jnp.where(live, starts, -1)
    lead = records.shape[2] - (smooth_taps.shape[0] - 1) // 2
    taps_row = jnp.pad(smooth_taps, (lead, 2 * WIDE - lead - smooth_taps.shape[0]))[None]
    middle, starts, taps_row = lax.optimization_barrier((middle, starts, taps_row))
    first_swap = swapped(middle, "cable", REACH, 1, [(last, 1)])
    second_swap = swapped(middle, "cable", REACH, 0)
    own = own_spectra(records, taps_row, tables[:2], share)
    products = far_products(starts, own, [first_swap, middle, second_swap], tables[2:])
    sent = lax.all_to_all(products, "pair", 0, 0)
    return place_lags(sent, rows).reshape(1, 1, 2 * LAG + 1, rows)


def solution(mesh):
    in_specs = (P("cable", "pair"), P(), P("cable", None), P("cable", None), P("cable"))
    out_specs = P("cable", "pair", None, None)
    return jax.shard_map(
        per_device, mesh=mesh, in_specs=in_specs, out_specs=out_specs, check_vma=False
    )
```
